32 devices in a mesh: space: 4 (over z), filt: 4 (over y, x), batch: 2 (over core).
Axes of the slice: x: 2, y: 2, z: 4, core: 2. Of those that a mesh axis runs over, the one named last changes fastest.
Arguments:
- features: bfloat16 [2, 72, 96, 2048], P('batch', 'space', None, 'filt'), may hold values from -6 to 6
- branch_preactivation: bfloat16 [2, 72, 96, 4, 256], P('batch', 'space', None, None, 'filt'), may hold values from -6 to 6
- cotangent: bfloat16 [2, 72, 96, 256], P('batch', 'space'), may hold values from -6 to 6
- pointwise_weight: bfloat16 [256, 2048], P('filt'), may hold values from -0.125 to 0.125
- dilated_weight: bfloat16 [3, 9, 256, 2048], P(None, None, 'filt'), may hold values from -0.0625 to 0.0625
- projection_weight: bfloat16 [4, 256, 256], P(None, 'filt'), may hold values from -0.1875 to 0.1875
Outputs:
- feature_gradient: bfloat16 [2, 72, 96, 2048], P('batch', 'space', None, 'filt')
- pointwise_weight_gradient: float32 [256, 2048], P('filt', ('space', 'batch'))
- dilated_weight_gradient: float32 [3, 9, 256, 2048], P(None, None, 'filt', ('space', 'batch'))
- projection_weight_gradient: float32 [4, 256, 256], P(None, 'filt', ('space', 'batch'))
The draws below stay inside these ranges and needn't reach their ends.
All inputs are finite; a program needn't handle non-finite values.
Results may differ from the reference program's by a relative error of at most 0.005.
Values may be sent and summed in bfloat16 or wider, within the bound.
A program may use at most 128 MiB of HBM per device.

```python
import jax
import jax.numpy as jnp
from jax import lax

INPUT_CHANNELS = 2048
BRANCH_FILTERS = 256
OUT = 256
WIDTH = 96
IMAGES = 2
HEIGHT = 72


def with_spikes(array, own_key, source, target, parts, factor):
    owner, partner = [(jnp.arange(array.shape[position]) // (array.shape[position] // parts)).reshape([-1 if axis == position else 1 for axis in range(array.ndim)]) for position in (source, target)]
    chosen = jax.random.permutation(own_key, parts)[partner]
    strong = (owner == chosen) | (owner == (partner + parts // 2) % parts)
    return jnp.where(strong, factor * array, array)


def level_of(own_key, extent, cuts, least, top_value):
    gain = 1.0
    for axis_at, blocks in cuts:
        steps = jax.random.uniform(jax.random.fold_in(jax.random.fold_in(own_key, 6), axis_at), (blocks,), jnp.float32, least / len(cuts), top_value / len(cuts))
        gain = gain * jnp.repeat(jnp.exp(steps), extent[axis_at] // blocks).reshape((-1,) + (1,) * (len(extent) - 1 - axis_at))
    return gain


def noise(own_key, dims, scale, reach, split=(), dtype=jnp.bfloat16):
    drawn = jax.random.normal(own_key, dims, jnp.float32) * scale
    if len(split) > 0:
        drawn = level_of(own_key, dims, split, -0.22, 0.18) * drawn
    return jnp.clip(drawn, min=-reach, max=reach).astype(dtype)


def gaussian_with(stream_key, shape, spread, most, split, heavy, dtype=jnp.bfloat16):
    result = spread * jax.random.normal(stream_key, shape, jnp.float32)
    if split:
        result = result * level_of(stream_key, shape, split, -0.22, 0.18)
    return jnp.clip(with_spikes(result, jax.random.fold_in(stream_key, 3), *heavy), -most, most).astype(dtype)


def setup_inputs(seed: int = 0) -> dict:
    splits = jax.random.split(jax.random.key(seed), 7)
    return {
        "features": noise(splits[0], (IMAGES, HEIGHT, WIDTH, INPUT_CHANNELS), 1.0, 6.0, ((0, 2), (1, 4), (3, 4))),
        "branch_preactivation": noise(splits[1], (IMAGES, HEIGHT, WIDTH, 4, BRANCH_FILTERS), 1.0, 6.0, ((0, 2), (1, 4), (4, 4))),
        "cotangent": noise(splits[2], (IMAGES, HEIGHT, WIDTH, OUT), 1.0, 6.0, ((0, 2), (1, 4))),
        "pointwise_weight": noise(splits[3], (BRANCH_FILTERS, INPUT_CHANNELS), INPUT_CHANNELS ** -0.5, 0.125, ((0, 4),)),
        "dilated_weight": gaussian_with(splits[4], (3, 9, BRANCH_FILTERS, INPUT_CHANNELS), (9 * INPUT_CHANNELS) ** -0.5, 0.0625, ((2, 4),), (2, 3, 4, 2.0)),
        "projection_weight": noise(splits[5], (4, BRANCH_FILTERS, OUT), (4 * BRANCH_FILTERS) ** -0.5, 0.1875, ((1, 4),)),
    }


dilations = (6, 12, 18)
dilation_extent = 18


def reference(features, branch_preactivation, cotangent, pointwise_weight, dilated_weight, projection_weight):
    image_count, image_height, image_width, channel_count = features.shape
    filter_count = pointwise_weight.shape[0]
    pixels = image_count * image_height * image_width
    gradient_scale = float(pixels) ** -0.5
    grad_cat = jnp.einsum('ihwo,bfo->ihwbf', cotangent.astype(jnp.float32), projection_weight.astype(jnp.float32))
    cot = jnp.where(branch_preactivation > 0, grad_cat, 0.0).astype(jnp.bfloat16)
    active = jnp.maximum(branch_preactivation, 0).astype(jnp.float32)
    projection_weight_gradient = jnp.einsum('ihwbf,ihwo->bfo', active, cotangent.astype(jnp.float32)) * gradient_scale
    cot_float = cot.astype(jnp.float32)
    flat = features.astype(jnp.float32).reshape(pixels, channel_count)
    point_slab = cot_float[:, :, :, 0, :].reshape(pixels, filter_count)
    feature_gradient = jnp.dot(point_slab, pointwise_weight.astype(jnp.float32), precision=lax.Precision.HIGHEST)
    pointwise_weight_gradient = jnp.dot(point_slab.T, flat, precision=lax.Precision.HIGHEST) * gradient_scale
    padded = jnp.pad(cot_float[:, :, :, 1:, :], ((0, 0), (dilation_extent, dilation_extent), (dilation_extent, dilation_extent), (0, 0), (0, 0)))
    gradient_list = []
    for branch_index in range(3):
        dilation = dilations[branch_index]
        for row_offset in range(3):
            for column_offset in range(3):
                row_start = dilation_extent - (row_offset - 1) * dilation
                col_start = dilation_extent - (column_offset - 1) * dilation
                slab = padded[:, row_start:row_start + image_height, col_start:col_start + image_width, branch_index, :]
                slab = slab.reshape(pixels, filter_count)
                weight_tensor = dilated_weight[branch_index, 3 * row_offset + column_offset].astype(jnp.float32)
                feature_gradient = feature_gradient + jnp.dot(slab, weight_tensor, precision=lax.Precision.HIGHEST)
                gradient_list.append(jnp.dot(slab.T, flat, precision=lax.Precision.HIGHEST))
    dilated_weight_gradient = jnp.stack(gradient_list).reshape(3, 9, filter_count, channel_count) * gradient_scale
    return feature_gradient.astype(jnp.bfloat16).reshape(image_count, image_height, image_width, channel_count), pointwise_weight_gradient, dilated_weight_gradient, projection_weight_gradient
```

```python
import functools

import jax
import jax.numpy as jnp
from jax import lax
from jax.experimental import pallas as pl
from jax.experimental.pallas import tpu as pltpu
from jax.sharding import PartitionSpec as P

dilations = (6, 12, 18)
dilation_extent = 18


def padded_2(x, sides, width):
    for axis, dim in sides:
        peers, length = (lax.axis_size(axis), x.shape[dim])
        up = [(i, (i + 1) % peers) for i in range(peers - 1)]
        down = [(j, i) for i, j in up]
        last = lax.slice_in_dim(x, length - width, length, axis=dim)
        initial = lax.slice_in_dim(x, 0, width, axis=dim)
        before = lax.ppermute(last, axis, up)
        after = lax.ppermute(initial, axis, down)
        x = jnp.concatenate([before, x, after], axis=dim)
    return x


def window(padded, branch_index, row_offset, column_offset, rows, cols):
    dilation = dilations[branch_index]
    row_start = dilation_extent - (row_offset - 1) * dilation
    col_start = dilation_extent - (column_offset - 1) * dilation
    return padded[:, row_start : row_start + rows, col_start : col_start + cols]


def plain_body(
    features, branch_preactivation, cotangent, pointwise_weight, dilated_weight, projection_weight
):
    image_count, rows, cols, cin_dev = features.shape
    filters_per_shard = pointwise_weight.shape[0]
    input_channels_total = pointwise_weight.shape[1]
    out_all = cotangent.shape[3]
    pixels = image_count * rows * cols
    flat_cot = cotangent.reshape(pixels, out_all)
    grad_cat = jnp.einsum(
        "po,bfo->pbf", flat_cot, projection_weight, preferred_element_type=jnp.float32
    )
    active_mask = branch_preactivation.reshape(pixels, 4, filters_per_shard) > 0
    cot = jnp.where(active_mask, grad_cat, 0.0).astype(jnp.bfloat16)
    active = jnp.maximum(branch_preactivation, 0).reshape(pixels, 4, filters_per_shard)
    proj_part = jnp.einsum("pbf,po->bfo", active, flat_cot, preferred_element_type=jnp.float32)
    branch_cotangents = cot.reshape(image_count, rows, cols, 4 * filters_per_shard)
    weight_collection = jnp.concatenate(
        [
            pointwise_weight[None],
            dilated_weight.reshape(27, filters_per_shard, input_channels_total),
        ],
        axis=0,
    )
    col_pad = ((0, 0), (0, 0), (dilation_extent, dilation_extent), (0, 0))
    cot_point = branch_cotangents[:, :, :, :filters_per_shard]
    dilated_cotangent = branch_cotangents[:, :, :, filters_per_shard:]
    border_padded = padded_2(dilated_cotangent, (("space", 1),), dilation_extent)
    padded = jnp.pad(border_padded, col_pad).reshape(
        image_count, rows + 2 * dilation_extent, cols + 2 * dilation_extent, 3, filters_per_shard
    )
    pieces = [cot_point]
    for branch_index in range(3):
        for row_offset in range(3):
            for column_offset in range(3):
                pieces.append(
                    window(padded, branch_index, row_offset, column_offset, rows, cols)[
                        :, :, :, branch_index
                    ]
                )
    stacked = jnp.concatenate(pieces, axis=3).reshape(pixels, 28 * filters_per_shard)
    weight_rows = weight_collection.reshape(28 * filters_per_shard, input_channels_total)
    summed = lax.psum_scatter(
        lax.dot_general(
            weight_rows, stacked, (((0,), (1,)), ((), ())), preferred_element_type=jnp.float32
        ),
        "filt",
        scatter_dimension=0,
        tiled=True,
    )
    feature_gradient = summed.T.astype(jnp.bfloat16).reshape(image_count, rows, cols, cin_dev)
    piece = lax.all_gather(features, "filt", axis=3, tiled=True)
    flat_piece = piece.reshape(pixels, piece.shape[3])
    conv_part = lax.dot_general(
        stacked, flat_piece, (((0,), (0,)), ((), ())), preferred_element_type=jnp.float32
    ).reshape(28, filters_per_shard, input_channels_total)
    gradient_scale = float(pixels * lax.axis_size("space") * lax.axis_size("batch")) ** (-0.5)
    pointwise_weight_sum, dilated_weight_sum, projection_weight_sum = (
        lax.psum_scatter(conv_part[0], ("space", "batch"), scatter_dimension=1, tiled=True),
        lax.psum_scatter(
            conv_part[1:].reshape(3, 9, filters_per_shard, input_channels_total),
            ("space", "batch"),
            scatter_dimension=3,
            tiled=True,
        ),
        lax.psum_scatter(proj_part, ("space", "batch"), scatter_dimension=2, tiled=True),
    )
    return (
        feature_gradient,
        pointwise_weight_sum * gradient_scale,
        dilated_weight_sum * gradient_scale,
        projection_weight_sum * gradient_scale,
    )


def slab_kernel(filters, point_ref, before_ref, own_ref, after_ref, out_ref, held):
    h = pl.program_id(0)
    rows, cols = own_ref.shape[0], own_ref.shape[1]

    @pl.when(h == 0)
    def _():
        held[0:dilation_extent] = before_ref[...].astype(jnp.float32)
        held[dilation_extent : dilation_extent + rows] = own_ref[...].astype(jnp.float32)
        held[dilation_extent + rows :] = after_ref[...].astype(jnp.float32)

    column = lax.broadcasted_iota(jnp.int32, (cols, filters), 0)
    parts = [point_ref[0].astype(jnp.float32)]
    for j, dilation in enumerate(dilations):
        for ky in range(3):
            line = held[h + dilation_extent - (ky - 1) * dilation]
            line = line[:, j * filters : (j + 1) * filters]
            for kx in range(3):
                shift = (kx - 1) * dilation
                if shift == 0:
                    parts.append(line)
                    continue
                moved = pltpu.roll(line, shift % cols, 0)
                inside = column >= shift if shift > 0 else column < cols + shift
                parts.append(jnp.where(inside, moved, 0.0))
    for i in range(0, len(parts), 2):
        pair = jnp.concatenate(parts[i : i + 2], axis=1)
        out_ref[:, i * filters : (i + 2) * filters] = pair.astype(jnp.bfloat16)


def build_slabs(point, before, own, after):
    rows, cols, filters = point.shape
    whole = lambda a: pl.BlockSpec(a.shape, lambda h: (0, 0, 0))
    return pl.pallas_call(
        functools.partial(slab_kernel, filters),
        grid=(rows,),
        in_specs=[
            pl.BlockSpec((1, cols, filters), lambda h: (h, 0, 0)),
            whole(before),
            whole(own),
            whole(after),
        ],
        out_specs=pl.BlockSpec((cols, 28 * filters), lambda h: (h, 0)),
        out_shape=jax.ShapeDtypeStruct((rows * cols, 28 * filters), jnp.bfloat16),
        scratch_shapes=[pltpu.VMEM((rows + 2 * dilation_extent, cols, 3 * filters), jnp.float32)],
        compiler_params=pltpu.CompilerParams(vmem_limit_bytes=40 * 1024 * 1024),
        cost_estimate=pl.CostEstimate(flops=0, bytes_accessed=30000000, transcendentals=0),
    )(point, before, own, after)


def dot(a, b, dims, dtype=jnp.float32):
    return lax.dot_general(a, b, (dims, ((), ())), preferred_element_type=jnp.float32).astype(dtype)


def f32(x):
    return x.astype(jnp.float32)


row_groups = 2


def body(
    features, branch_preactivation, cotangent, pointwise_weight, dilated_weight, projection_weight
):
    _, rows, cols, cin_dev = features.shape
    filters = pointwise_weight.shape[0]
    out_all = cotangent.shape[3]
    pixels = rows * cols
    half = cin_dev // 2
    space_count = lax.axis_size("space")
    z, q, b = lax.axis_index("space"), lax.axis_index("filt"), lax.axis_index("batch")
    over_x = lambda a: lax.ppermute(a, "filt", [(i, i ^ 1) for i in range(4)])
    over_y = lambda a: lax.ppermute(a, "filt", [(i, i ^ 2) for i in range(4)])
    over_core = lambda a: lax.ppermute(a, "batch", [(0, 1), (1, 0)])

    flat = features.reshape(pixels, cin_dev)
    own_a = lax.dynamic_slice_in_dim(flat, b * half, half, axis=1)
    own_b = lax.dynamic_slice_in_dim(flat, (1 - b) * half, half, axis=1)
    fa, fb = {0: own_a}, {0: own_b}
    fa[1] = over_x(own_a)
    fb[2] = over_y(own_b)
    fa[2] = over_y(own_a)
    fb[1] = over_x(own_b)
    fa[3] = over_y(fa[1])
    fb[3] = over_x(fb[2])

    flat_cot = cotangent.reshape(pixels, out_all)
    pre = branch_preactivation.reshape(pixels, 4 * filters)
    proj = projection_weight.reshape(4 * filters, out_all)
    grad_cat = dot(flat_cot, proj, ((1,), (1,)))
    cot = jnp.where(pre > 0, grad_cat, 0.0).astype(jnp.bfloat16)
    point = cot[:, :filters].reshape(rows, cols, filters)
    own = cot[:, filters:].reshape(rows, cols, 3 * filters)
    up = [(i, i + 1) for i in range(space_count - 1)]
    down = [(j, i) for i, j in up]
    before = lax.ppermute(own[rows - dilation_extent :], "space", up)
    after = lax.ppermute(own[:dilation_extent], "space", down)
    stacked = build_slabs(point, before, own, after)
    proj_part = dot(jnp.maximum(pre, 0), flat_cot, ((0,), (0,))).reshape(4, filters, out_all)
    proj_sum = lax.psum_scatter(
        proj_part, ("space", "batch"), scatter_dimension=2, tiled=True
    )

    dil = dilated_weight.reshape(27 * filters, 4 * cin_dev)

    def input_part(r, dtype):
        start = (q ^ r) * cin_dev
        weights = jnp.concatenate(
            [lax.dynamic_slice_in_dim(w, start, cin_dev, axis=1) for w in (pointwise_weight, dil)]
        )
        return dot(stacked, weights, ((1,), (0,)), dtype)

    d1, d2, d3 = [input_part(r, jnp.bfloat16) for r in (1, 2, 3)]
    d0 = input_part(0, jnp.float32)

    row_count = 28 * filters // row_groups
    groups = []
    for g in range(row_groups):
        lhs = stacked[:, g * row_count : (g + 1) * row_count]
        sent = {r: over_core(dot(lhs, fb[r], ((0,), (0,)), jnp.bfloat16)) for r in range(4)}
        sums = [
            (dot(lhs, fa[r], ((0,), (0,))) + f32(sent[r])).astype(jnp.bfloat16) for r in range(4)
        ]
        groups.append(jnp.stack(sums))

    d1, d2, d3, fa[3], fb[3], fa[2], fb[1] = lax.optimization_barrier(
        (d1, d2, d3, fa[3], fb[3], fa[2], fb[1])
    )
    cut = pixels // 2
    got_a1, got_a3 = over_x(d1[:cut]), over_x(d3[:cut])
    got_b2, got_b3 = over_y(d2[cut:]), over_y(d3[cut:])
    mid_a = (f32(d2[:cut]) + f32(got_a3)).astype(jnp.bfloat16)
    mid_b = (f32(d1[cut:]) + f32(got_b3)).astype(jnp.bfloat16)
    last_a, last_b = over_y(mid_a), over_x(mid_b)
    feature_gradient = jnp.concatenate(
        [
            (d0[:cut] + f32(got_a1) + f32(last_a)).astype(jnp.bfloat16),
            (d0[cut:] + f32(got_b2) + f32(last_b)).astype(jnp.bfloat16),
        ]
    ).reshape(1, rows, cols, cin_dev)

    n = space_count
    pick = lambda s, d: lax.dynamic_index_in_dim(s, jnp.clip(d, 0, n - 1) ^ q, 0, keepdims=False)
    right, left = [None] * row_groups, [None] * row_groups
    for k in range(1, n):
        ups = [(i, i + 1) for i in range(k)]
        downs = [(n - 1 - i, n - 2 - i) for i in range(k)]
        for g in range(row_groups):
            a, c = pick(groups[g], n - k + z), pick(groups[g], z - n + k)
            if k > 1:
                a = (f32(a) + f32(right[g])).astype(jnp.bfloat16)
                c = (f32(c) + f32(left[g])).astype(jnp.bfloat16)
            right[g], left[g] = lax.ppermute(a, "space", ups), lax.ppermute(c, "space", downs)
    scale = float(pixels * n * lax.axis_size("batch")) ** (-0.5)
    total = jnp.concatenate(
        [
            (f32(pick(groups[g], z)) + f32(right[g]) + f32(left[g])) * scale
            for g in range(row_groups)
        ]
    )
    return (
        feature_gradient,
        total[:filters],
        total[filters:].reshape(3, 9, filters, half),
        proj_sum * scale,
    )


def solution(mesh):
    sizes = (mesh.shape["space"], mesh.shape["filt"], mesh.shape["batch"])
    return jax.shard_map(
        body if sizes == (4, 4, 2) else plain_body,
        mesh=mesh,
        in_specs=(
            P("batch", "space", None, "filt"),
            P("batch", "space", None, None, "filt"),
            P("batch", "space", None, None),
            P("filt", None),
            P(None, None, "filt", None),
            P(None, "filt", None),
        ),
        out_specs=(
            P("batch", "space", None, "filt"),
            P("filt", ("space", "batch")),
            P(None, None, "filt", ("space", "batch")),
            P(None, "filt", ("space", "batch")),
        ),
        check_vma=False,
    )
```

```python
import functools

import jax
import jax.numpy as jnp
from jax import lax
from jax.experimental import pallas as pl
from jax.experimental.pallas import tpu as pltpu
from jax.sharding import PartitionSpec as P

dilations = (6, 12, 18)
dilation_extent = 18


def padded_2(x, sides, width):
    for axis, dim in sides:
        peers, length = (lax.axis_size(axis), x.shape[dim])
        up = [(i, (i + 1) % peers) for i in range(peers - 1)]
        down = [(j, i) for i, j in up]
        last = lax.slice_in_dim(x, length - width, length, axis=dim)
        initial = lax.slice_in_dim(x, 0, width, axis=dim)
        before = lax.ppermute(last, axis, up)
        after = lax.ppermute(initial, axis, down)
        x = jnp.concatenate([before, x, after], axis=dim)
    return x


def window(padded, branch_index, row_offset, column_offset, rows, cols):
    dilation = dilations[branch_index]
    row_start = dilation_extent - (row_offset - 1) * dilation
    col_start = dilation_extent - (column_offset - 1) * dilation
    return padded[:, row_start : row_start + rows, col_start : col_start + cols]


def plain_body(
    features, branch_preactivation, cotangent, pointwise_weight, dilated_weight, projection_weight
):
    image_count, rows, cols, cin_dev = features.shape
    filters_per_shard = pointwise_weight.shape[0]
    input_channels_total = pointwise_weight.shape[1]
    out_all = cotangent.shape[3]
    pixels = image_count * rows * cols
    flat_cot = cotangent.reshape(pixels, out_all)
    grad_cat = jnp.einsum(
        "po,bfo->pbf", flat_cot, projection_weight, preferred_element_type=jnp.float32
    )
    active_mask = branch_preactivation.reshape(pixels, 4, filters_per_shard) > 0
    cot = jnp.where(active_mask, grad_cat, 0.0).astype(jnp.bfloat16)
    active = jnp.maximum(branch_preactivation, 0).reshape(pixels, 4, filters_per_shard)
    proj_part = jnp.einsum("pbf,po->bfo", active, flat_cot, preferred_element_type=jnp.float32)
    branch_cotangents = cot.reshape(image_count, rows, cols, 4 * filters_per_shard)
    weight_collection = jnp.concatenate(
        [
            pointwise_weight[None],
            dilated_weight.reshape(27, filters_per_shard, input_channels_total),
        ],
        axis=0,
    )
    col_pad = ((0, 0), (0, 0), (dilation_extent, dilation_extent), (0, 0))
    cot_point = branch_cotangents[:, :, :, :filters_per_shard]
    dilated_cotangent = branch_cotangents[:, :, :, filters_per_shard:]
    border_padded = padded_2(dilated_cotangent, (("space", 1),), dilation_extent)
    padded = jnp.pad(border_padded, col_pad).reshape(
        image_count, rows + 2 * dilation_extent, cols + 2 * dilation_extent, 3, filters_per_shard
    )
    pieces = [cot_point]
    for branch_index in range(3):
        for row_offset in range(3):
            for column_offset in range(3):
                pieces.append(
                    window(padded, branch_index, row_offset, column_offset, rows, cols)[
                        :, :, :, branch_index
                    ]
                )
    stacked = jnp.concatenate(pieces, axis=3).reshape(pixels, 28 * filters_per_shard)
    weight_rows = weight_collection.reshape(28 * filters_per_shard, input_channels_total)
    summed = lax.psum_scatter(
        lax.dot_general(
            weight_rows, stacked, (((0,), (1,)), ((), ())), preferred_element_type=jnp.float32
        ),
        "filt",
        scatter_dimension=0,
        tiled=True,
    )
    feature_gradient = summed.T.astype(jnp.bfloat16).reshape(image_count, rows, cols, cin_dev)
    piece = lax.all_gather(features, "filt", axis=3, tiled=True)
    flat_piece = piece.reshape(pixels, piece.shape[3])
    conv_part = lax.dot_general(
        stacked, flat_piece, (((0,), (0,)), ((), ())), preferred_element_type=jnp.float32
    ).reshape(28, filters_per_shard, input_channels_total)
    gradient_scale = float(pixels * lax.axis_size("space") * lax.axis_size("batch")) ** (-0.5)
    pointwise_weight_sum, dilated_weight_sum, projection_weight_sum = (
        lax.psum_scatter(conv_part[0], ("space", "batch"), scatter_dimension=1, tiled=True),
        lax.psum_scatter(
            conv_part[1:].reshape(3, 9, filters_per_shard, input_channels_total),
            ("space", "batch"),
            scatter_dimension=3,
            tiled=True,
        ),
        lax.psum_scatter(proj_part, ("space", "batch"), scatter_dimension=2, tiled=True),
    )
    return (
        feature_gradient,
        pointwise_weight_sum * gradient_scale,
        dilated_weight_sum * gradient_scale,
        projection_weight_sum * gradient_scale,
    )


def slab_kernel(filters, point_ref, before_ref, own_ref, after_ref, out_ref, held):
    h = pl.program_id(0)
    rows, cols = own_ref.shape[0], own_ref.shape[1]

    @pl.when(h == 0)
    def _():
        held[0:dilation_extent] = before_ref[...].astype(jnp.float32)
        held[dilation_extent : dilation_extent + rows] = own_ref[...].astype(jnp.float32)
        held[dilation_extent + rows :] = after_ref[...].astype(jnp.float32)

    column = lax.broadcasted_iota(jnp.int32, (cols, filters), 0)
    parts = [point_ref[0].astype(jnp.float32)]
    for j, dilation in enumerate(dilations):
        for ky in range(3):
            line = held[h + dilation_extent - (ky - 1) * dilation]
            line = line[:, j * filters : (j + 1) * filters]
            for kx in range(3):
                shift = (kx - 1) * dilation
                if shift == 0:
                    parts.append(line)
                    continue
                moved = pltpu.roll(line, shift % cols, 0)
                inside = column >= shift if shift > 0 else column < cols + shift
                parts.append(jnp.where(inside, moved, 0.0))
    for i in range(0, len(parts), 2):
        pair = jnp.concatenate(parts[i : i + 2], axis=1)
        out_ref[:, i * filters : (i + 2) * filters] = pair.astype(jnp.bfloat16)


def build_slabs(point, before, own, after):
    rows, cols, filters = point.shape
    whole = lambda a: pl.BlockSpec(a.shape, lambda h: (0, 0, 0))
    return pl.pallas_call(
        functools.partial(slab_kernel, filters),
        grid=(rows,),
        in_specs=[
            pl.BlockSpec((1, cols, filters), lambda h: (h, 0, 0)),
            whole(before),
            whole(own),
            whole(after),
        ],
        out_specs=pl.BlockSpec((cols, 28 * filters), lambda h: (h, 0)),
        out_shape=jax.ShapeDtypeStruct((rows * cols, 28 * filters), jnp.bfloat16),
        scratch_shapes=[pltpu.VMEM((rows + 2 * dilation_extent, cols, 3 * filters), jnp.float32)],
        compiler_params=pltpu.CompilerParams(vmem_limit_bytes=40 * 1024 * 1024),
        cost_estimate=pl.CostEstimate(flops=0, bytes_accessed=30000000, transcendentals=0),
    )(point, before, own, after)


def dot(a, b, dims, dtype=jnp.float32):
    return lax.dot_general(a, b, (dims, ((), ())), preferred_element_type=jnp.float32).astype(dtype)


def f32(x):
    return x.astype(jnp.float32)


column_groups = 2


def body(
    features, branch_preactivation, cotangent, pointwise_weight, dilated_weight, projection_weight
):
    _, rows, cols, cin_dev = features.shape
    filters = pointwise_weight.shape[0]
    out_all = cotangent.shape[3]
    pixels = rows * cols
    half = cin_dev // 2
    space_count = lax.axis_size("space")
    z, q, b = lax.axis_index("space"), lax.axis_index("filt"), lax.axis_index("batch")
    over_x = lambda a: lax.ppermute(a, "filt", [(i, i ^ 1) for i in range(4)])
    over_y = lambda a: lax.ppermute(a, "filt", [(i, i ^ 2) for i in range(4)])
    over_core = lambda a: lax.ppermute(a, "batch", [(0, 1), (1, 0)])

    flat = features.reshape(pixels, cin_dev)
    wide = half // column_groups
    own_columns = [
        [
            lax.dynamic_slice_in_dim(flat, c * half + g * wide, wide, axis=1)
            for c in (b, 1 - b)
        ]
        for g in range(column_groups)
    ]
    gathered = []
    for g in range(column_groups):
        own_a, own_b = own_columns[g]
        if g > 0:
            own_a, own_b, *gathered[-1] = lax.optimization_barrier(
                (own_a, own_b, *gathered[-1])
            )
        a1, b2 = over_x(own_a), over_y(own_b)
        a2, b1 = over_y(own_a), over_x(own_b)
        a3, b3 = over_y(a1), over_x(b2)
        gathered.append([own_a, a1, a2, a3, own_b, b1, b2, b3])

    flat_cot = cotangent.reshape(pixels, out_all)
    pre = branch_preactivation.reshape(pixels, 4 * filters)
    proj = projection_weight.reshape(4 * filters, out_all)
    grad_cat = dot(flat_cot, proj, ((1,), (1,)))
    cot = jnp.where(pre > 0, grad_cat, 0.0).astype(jnp.bfloat16)
    point = cot[:, :filters].reshape(rows, cols, filters)
    own = cot[:, filters:].reshape(rows, cols, 3 * filters)
    up = [(i, i + 1) for i in range(space_count - 1)]
    down = [(j, i) for i, j in up]
    before = lax.ppermute(own[rows - dilation_extent :], "space", up)
    after = lax.ppermute(own[:dilation_extent], "space", down)
    stacked = build_slabs(point, before, own, after)
    proj_part = dot(jnp.maximum(pre, 0), flat_cot, ((0,), (0,)))
    share = out_all // (2 * space_count)
    proj_rows = 4 * filters * share // wide
    split = proj_part.reshape(proj_rows, wide // share, 2, 2, 2, share)
    split = jnp.where(q >= 2, split[:, :, ::-1], split)
    split = jnp.where(q % 2 == 1, split[:, :, :, ::-1], split)
    split = split.transpose(4, 0, 2, 3, 1, 5).reshape(2, proj_rows, space_count * wide)
    proj_sums = jnp.where(b == 0, split[0], split[1]) + over_core(
        jnp.where(b == 0, split[1], split[0])
    )

    dil = dilated_weight.reshape(27 * filters, 4 * cin_dev)

    def input_part(r, dtype):
        start = (q ^ r) * cin_dev
        weights = jnp.concatenate(
            [lax.dynamic_slice_in_dim(w, start, cin_dev, axis=1) for w in (pointwise_weight, dil)]
        )
        return dot(stacked, weights, ((1,), (0,)), dtype)

    d1, d2, d3 = [input_part(r, jnp.bfloat16) for r in (1, 2, 3)]
    d0 = input_part(0, jnp.float32)

    groups = []
    for g in range(column_groups):
        a = jnp.concatenate(gathered[g][:4], axis=1)
        c = jnp.concatenate(gathered[g][4:], axis=1)
        sent = over_core(dot(stacked, c, ((0,), (0,)), jnp.bfloat16))
        sums = dot(stacked, a, ((0,), (0,))) + f32(sent)
        sums = sums.astype(jnp.bfloat16)
        if g == 0:
            sums = jnp.concatenate([sums, proj_sums.astype(jnp.bfloat16)])
        groups.append(sums)

    d1, d2, d3, *_ = lax.optimization_barrier((d1, d2, d3, *gathered[-1]))
    cut = pixels // 2
    got_a3, got_b3 = over_x(d3[:cut]), over_y(d3[cut:])
    near_a, near_b, got_a3, got_b3 = lax.optimization_barrier(
        (d1[:cut], d2[cut:], got_a3, got_b3)
    )
    got_a1, got_b2 = over_x(near_a), over_y(near_b)
    mid_a = (f32(d2[:cut]) + f32(got_a3)).astype(jnp.bfloat16)
    mid_b = (f32(d1[cut:]) + f32(got_b3)).astype(jnp.bfloat16)
    last_a, last_b = over_y(mid_a), over_x(mid_b)
    feature_gradient = jnp.concatenate(
        [
            (d0[:cut] + f32(got_a1) + f32(last_a)).astype(jnp.bfloat16),
            (d0[cut:] + f32(got_b2) + f32(last_b)).astype(jnp.bfloat16),
        ]
    ).reshape(1, rows, cols, cin_dev)

    n = space_count
    pick = lambda s, d: lax.dynamic_slice_in_dim(
        s, (jnp.clip(d, 0, n - 1) ^ q) * wide, wide, axis=1
    )
    right, left = [None] * column_groups, [None] * column_groups
    for g in range(column_groups):
        for k in range(1, n):
            ups = [(i, i + 1) for i in range(k)]
            downs = [(n - 1 - i, n - 2 - i) for i in range(k)]
            a, c = pick(groups[g], n - k + z), pick(groups[g], z - n + k)
            if k > 1:
                a = (f32(a) + f32(right[g])).astype(jnp.bfloat16)
                c = (f32(c) + f32(left[g])).astype(jnp.bfloat16)
            right[g], left[g] = lax.ppermute(a, "space", ups), lax.ppermute(c, "space", downs)
    scale = float(pixels * n * lax.axis_size("batch")) ** (-0.5)
    totals = [
        (f32(pick(groups[g], z)) + f32(right[g]) + f32(left[g])) * scale
        for g in range(column_groups)
    ]
    kept = 28 * filters
    total = jnp.concatenate([t[:kept] for t in totals], axis=1)
    return (
        feature_gradient,
        total[:filters],
        total[filters:].reshape(3, 9, filters, half),
        totals[0][kept:].reshape(4, filters, share),
    )


def solution(mesh):
    sizes = (mesh.shape["space"], mesh.shape["filt"], mesh.shape["batch"])
    return jax.shard_map(
        body if sizes == (4, 4, 2) else plain_body,
        mesh=mesh,
        in_specs=(
            P("batch", "space", None, "filt"),
            P("batch", "space", None, None, "filt"),
            P("batch", "space", None, None),
            P("filt", None),
            P(None, None, "filt", None),
            P(None, "filt", None),
        ),
        out_specs=(
            P("batch", "space", None, "filt"),
            P("filt", ("space", "batch")),
            P(None, None, "filt", ("space", "batch")),
            P(None, "filt", ("space", "batch")),
        ),
        check_vma=False,
    )
```
